512 devices in a mesh: ctx: 16 (over z), head: 8 (over x, y_hi), pack: 4 (over y_lo, core).
Axes of the slice: x: 4, y: 4 (y_hi: 2, y_lo: 2; y = y_hi * 2 + y_lo), z: 16, core: 2. Of those that a mesh axis runs over, the one named last changes fastest.
Arguments:
- queries: bfloat16 [2048, 16384], P(('pack', 'ctx'), 'head'), parts along dimension 0, may hold values from -12 to 12
- cached_keys: bfloat16 [65536, 1024], P(('pack', 'ctx'), 'head'), parts along dimension 0, may hold values from -6 to 6
- cached_values: bfloat16 [65536, 1024], P(('pack', 'ctx'), 'head'), parts along dimension 0, may hold values from -15 to 15
- turn_lengths: int32 [32], P('pack'), parts along dimension 0, may hold values from 1 to 128, 512 in all
- tile_map: int32 [32, 16], P('pack'), parts along dimension 0, may hold values from 0 to 1, as said below
- prefix_len: int32 [64], P('pack'), parts along dimension 0, may hold values from 2 to 1024, as said below
- owner_ids: int32 [64], P('pack'), parts along dimension 0, may hold values from 0 to 15, each once
Outputs:
- attended: bfloat16 [2048, 16384], P(('pack', 'ctx'), 'head'), parts along dimension 0
The draws below stay inside these ranges and needn't reach their ends.
There are 4 independent parts, one for each index of `pack`. The reference program is written for one: setup_inputs(seed, part) draws one part's arguments, and reference() takes and returns one part's arrays. A program takes and returns all parts, laid end to end along the dimension named above; each array names one. Nothing has to cross between parts.
Inputs may be any that keep to these rules, and one draw needn't show every extreme that they name: `turn_lengths`: every turn is 1 row or more and they sum to 512. `tile_map`: every turn sees at least one cache shard. `prefix_len`: some shard is full. `owner_ids`: a permutation of 0..15.
All inputs are finite; a program needn't handle non-finite values.
Results may differ from the reference program's by a relative error of at most 0.0052.
Values may be sent and summed in bfloat16 or wider, within the bound.
A program may use at most 64 MiB of HBM per device.

```python
import math
import jax
import jax.numpy as jnp
import numpy as np
from jax import lax

QH = 128
KVH = 8
HD = 128
Q_DEV = 32
CACHE_DEV = 1024
NTURN = 8
NEW = 512
CACHE = 16384
N_CTX = 16


def draw_queries(key, part):
    key = jax.random.fold_in(key, 11)
    first = jax.random.fold_in(key, 0)
    shape = (Q_DEV * N_CTX, QH * HD)
    base = jnp.clip(2.0 * jax.random.normal(first, shape, jnp.float32), -12.0, 12.0)
    return base.astype(jnp.bfloat16)


def draw_cached_keys(key, part):
    key = jax.random.fold_in(key, 13)
    shape = (CACHE_DEV * N_CTX, KVH * HD)
    base = jnp.clip(jax.random.normal(key, shape, jnp.float32), -6.0, 6.0)
    return base.astype(jnp.bfloat16)


def draw_tile_map(key, part):
    key = jax.random.fold_in(key, 17)
    first, second = jax.random.split(key)
    coins = jax.random.randint(first, (NTURN, N_CTX), 0, 2)
    forced = jax.random.randint(second, (NTURN,), 0, N_CTX)
    columns = jnp.arange(N_CTX, dtype=jnp.int32)
    return jnp.maximum(coins, (columns[None, :] == forced[:, None]).astype(jnp.int32)).astype(jnp.int32)


def draw_prefix_len(key, part):
    key = jax.random.fold_in(key, 19)
    first, second = jax.random.split(key)
    lengths = jax.random.randint(first, (N_CTX,), 2, CACHE_DEV + 1)
    full_one = jax.random.randint(second, (), 0, N_CTX)
    shards = jnp.arange(N_CTX, dtype=jnp.int32)
    return jnp.where(shards == full_one, CACHE_DEV, lengths).astype(jnp.int32)


def steps_of(rng, extent, cuts, smallest, high):
    def one(dim, parts):
        steps = jax.random.uniform(jax.random.fold_in(jax.random.fold_in(rng, 6), dim), (parts,), jnp.float32, smallest / len(cuts), high / len(cuts))
        return jnp.repeat(jnp.exp(steps), extent[dim] // parts).reshape((-1,) + (1,) * (len(extent) - dim - 1))

    gain = one(*cuts[0])
    for cut in cuts[1:]:
        gain = gain * one(*cut)
    return gain


def length_profile(count, total, bound, lean):
    loads = [(1 << 20) // math.isqrt(standing ** lean) + 1 for standing in range(2, count + 1)]
    surplus, counts = total - bound - (count - 1), [1] * (count - 1)
    while surplus > 0:
        movable = [i for i in range(count - 1) if counts[i] < bound]
        whole, left = sum([loads[i] for i in movable]), surplus
        for i in movable:
            extra = min(bound - counts[i], max(1, left * loads[i] // whole), surplus)
            counts[i] = counts[i] + extra
            surplus = surplus - extra
    return np.array([bound] + counts)


def ragged(rng, amount, total, reach, skew):
    if amount == 2:
        one = jax.random.randint(rng, (), max(1, total - reach), min(reach, total - 1) + 1)
        return jnp.stack([one, total - one])
    sizes = jnp.asarray(length_profile(amount, total, reach, skew), jnp.int32)
    twos = (amount - 1) // 2
    donor, sink = sizes[1:1 + 2 * twos:2], sizes[2:2 + 2 * twos:2]
    margin = jnp.minimum(donor - 1, reach - sink)
    moved = jax.random.randint(jax.random.fold_in(rng, 1), (twos,), 0, 1 << 20) % (margin + 1)
    sizes = sizes.at[1:1 + 2 * twos:2].set(donor - moved).at[2:2 + 2 * twos:2].set(sink + moved)
    return sizes[jax.random.permutation(jax.random.fold_in(rng, 2), amount)]


def centred(key, dims, width, limit, cuts=(), kind=jnp.bfloat16):
    values = width * jax.random.normal(key, dims, jnp.float32)
    if cuts:
        values = values * steps_of(key, dims, cuts, -0.22, 0.18)
    return jnp.clip(values, -limit, limit).astype(kind)


def setup_inputs(seed: int = 0, part: int = 0) -> dict:
    splits = jax.random.split(jax.random.key(seed), 8)
    part_splits = jax.random.split(jax.random.fold_in(splits[7], part), 8)
    queries = draw_queries(jax.random.fold_in(jax.random.fold_in(splits[7], part), 71), part)
    cached_keys = draw_cached_keys(jax.random.fold_in(jax.random.fold_in(splits[7], part), 71), part)
    cached_values = centred(part_splits[2], (CACHE, KVH * HD), 3.0, 15.0, ((0, 16), (1, 8)))
    turn_lengths = ragged(part_splits[3], NTURN, NEW, NEW // 4, 2).astype(jnp.int32)
    tile_map = draw_tile_map(jax.random.fold_in(jax.random.fold_in(splits[7], part), 71), part)
    prefix_len = draw_prefix_len(jax.random.fold_in(jax.random.fold_in(splits[7], part), 71), part)
    owner_ids = jax.random.permutation(part_splits[6], N_CTX).astype(jnp.int32)
    return {"queries": queries, "cached_keys": cached_keys, "cached_values": cached_values, "turn_lengths": turn_lengths, "tile_map": tile_map, "prefix_len": prefix_len, "owner_ids": owner_ids}


NEG = -1e30


def reference(queries, cached_keys, cached_values, turn_lengths, tile_map, prefix_len, owner_ids):
    total_rows = queries.shape[0]
    groups = cached_keys.shape[1] // HD
    query = queries.astype(jnp.float32).reshape(total_rows, groups, -1, HD)
    heads = query.shape[1] * query.shape[2]
    key_tiles = cached_keys.astype(jnp.float32).reshape(N_CTX, CACHE_DEV, groups, HD)
    value_tiles = cached_values.astype(jnp.float32).reshape(N_CTX, CACHE_DEV, groups, HD)
    ends = jnp.cumsum(turn_lengths)
    positions = jnp.arange(total_rows, dtype=jnp.int32)
    turns = jnp.sum((positions[:, None] >= ends[None, :]).astype(jnp.int32), axis=1)

    def absorb(state, item):
        shard, key_tile, value_tile = item
        peak_run, total_run, accum = state
        row_seen = tile_map[turns, shard] > 0
        key_live = jnp.arange(CACHE_DEV, dtype=jnp.int32) < prefix_len[shard]
        scores = jnp.einsum("qgjd,kgd->gjqk", query, key_tile) * (HD ** -0.5)
        mask = row_seen[None, None, :, None] & key_live[None, None, None, :]
        peak = jnp.max(jnp.where(mask, scores, NEG), axis=3)
        weights = jnp.where(mask, jnp.exp(scores - peak[..., None]), 0.0)
        total = jnp.maximum(jnp.sum(weights, axis=3), 1.0)
        weights_b = lax.optimization_barrier(weights.astype(jnp.bfloat16))
        mixed = jnp.einsum("gjqk,kgd->qgjd", weights_b.astype(jnp.float32), value_tile)
        mixed = (mixed / jnp.transpose(total, (2, 0, 1))[..., None]).astype(jnp.bfloat16)
        mixed = mixed.astype(jnp.float32).reshape(total_rows, heads, HD)
        spread = jnp.transpose(peak + jnp.log(total), (2, 0, 1)).reshape(total_rows, heads)
        new_peak = jnp.maximum(peak_run, spread)
        older = jnp.exp(peak_run - new_peak)
        fresh = jnp.exp(spread - new_peak)
        total_run = total_run * older + fresh
        accum = accum * older[..., None] + fresh[..., None] * mixed
        return (new_peak, total_run, accum), None

    start = (jnp.full((total_rows, heads), NEG, jnp.float32), jnp.zeros((total_rows, heads), jnp.float32),
             jnp.zeros((total_rows, heads, HD), jnp.float32))
    final, _ = lax.scan(absorb, start, (jnp.arange(N_CTX, dtype=jnp.int32), key_tiles, value_tiles))
    result = (final[2] / final[1][..., None]).reshape(total_rows, -1).astype(jnp.bfloat16)
    order = jnp.argsort(owner_ids)
    blocks = result.reshape(N_CTX, total_rows // N_CTX, -1)
    return jnp.take(blocks, order, axis=0).reshape(total_rows, -1)
```

```python
import math

import jax
import jax.numpy as jnp
from jax import lax
from jax.experimental import pallas as pl
from jax.experimental.pallas import tpu as pltpu
from jax.sharding import PartitionSpec as P

HD = 128
NEG = -1e30
MESH = pl.DeviceIdType.MESH
CHUNKS = 4
RIGHT, LEFT = 0, 1


def kernel(
    queries, cached_keys, cached_values, turn_lengths, tile_map, prefix_len, owner_ids,
    result,
    blocks, partials, spreads, keys, values, key_cols, value_cols, inverse, merged,
    arrived, leaving, arrived_spread, leaving_spread,
    load_sem, gather_send, gather_recv, part_send, part_recv, spread_send, spread_recv, store_sem,
):
    n = blocks.shape[0]
    rows = blocks.shape[2]
    width = blocks.shape[3]
    per_chunk = width // HD
    groups = rows // 8
    heads = CHUNKS * per_chunk
    cache = keys.shape[0]
    turns = turn_lengths.shape[0]
    reach = n // 2
    half = CHUNKS // 2
    me = lax.axis_index("ctx")
    right, left = lax.rem(me + 1, n), lax.rem(me + n - 1, n)
    to = ({"ctx": right}, {"ctx": left})
    scale2 = HD ** (-0.5) * math.log2(math.e)

    def place(offset):
        return lax.rem(me + offset + n, n)

    def chunk_of(side, position):
        return position if side == RIGHT else CHUNKS - 1 - position

    key_load = pltpu.make_async_copy(cached_keys, keys, load_sem.at[CHUNKS])
    value_load = pltpu.make_async_copy(cached_values, values, load_sem.at[CHUNKS + 1])
    own_loads = [
        pltpu.make_async_copy(
            queries.at[:, pl.ds(c * width, width)], blocks.at[me, c], load_sem.at[c]
        )
        for c in range(CHUNKS)
    ]
    for load in own_loads:
        load.start()
    key_load.start()
    value_load.start()

    barrier = pltpu.get_barrier_semaphore()
    for side in (RIGHT, LEFT):
        pl.semaphore_signal(barrier, inc=1, device_id=to[side], device_id_type=MESH)
    pl.semaphore_wait(barrier, 2)

    def gather_copy(side, step, block, c):
        return pltpu.make_async_remote_copy(
            src_ref=blocks.at[block, c],
            dst_ref=blocks.at[block, c],
            send_sem=gather_send.at[side, step, c],
            recv_sem=gather_recv.at[side, step, c],
            device_id=to[side],
            device_id_type=MESH,
        )

    def part_copy(side, step, c):
        return pltpu.make_async_remote_copy(
            src_ref=leaving.at[side, step, c],
            dst_ref=arrived.at[side, step, c],
            send_sem=part_send.at[side, step, c],
            recv_sem=part_recv.at[side, step, c],
            device_id=to[side],
            device_id_type=MESH,
        )

    def spread_copy(side, step):
        return pltpu.make_async_remote_copy(
            src_ref=leaving_spread.at[side, step],
            dst_ref=arrived_spread.at[side, step],
            send_sem=spread_send.at[side, step],
            recv_sem=spread_recv.at[side, step],
            device_id=to[side],
            device_id_type=MESH,
        )

    for load in own_loads:
        load.wait()
    for position in range(CHUNKS):
        for side in (RIGHT, LEFT):
            gather_copy(side, 0, me, chunk_of(side, position)).start()

    for owner in range(n):
        source = jnp.int32(0)
        for b in range(n):
            source = jnp.maximum(source, jnp.where(owner_ids[b] == owner, b, 0))
        inverse[owner] = source
    limit = prefix_len[me]
    bounds = []
    begin = jnp.int32(0)
    for t in range(turns):
        end = begin + turn_lengths[t]
        bounds.append((begin, end, tile_map[t, me]))
        begin = end

    key_load.wait()
    value_load.wait()
    live = lax.broadcasted_iota(jnp.int32, (cache, HD), 0) < limit
    key_all = keys[...].astype(jnp.float32)
    key_all = jnp.where(live, key_all, jnp.broadcast_to(key_all[0:1, :], (cache, HD)))
    key_cols[...] = key_all.T.astype(jnp.bfloat16)
    value_cols[:, 0:HD] = jnp.where(live, values[...].astype(jnp.float32), 0.0).astype(jnp.bfloat16)
    value_cols[:, HD:2 * HD] = jnp.where(live, 1.0, 0.0).astype(jnp.bfloat16)

    lane = lax.broadcasted_iota(jnp.int32, (8, HD), 1)
    sublane = lax.broadcasted_iota(jnp.int32, (8, HD), 0)

    def compute(pairs):
        query = jnp.concatenate(
            [
                blocks[block, c, :, pl.ds(j * HD, HD)]
                for block, c in pairs
                for j in range(per_chunk)
            ],
            axis=0,
        )
        scores = jnp.dot(query, key_cols[...], preferred_element_type=jnp.float32)
        peak = jnp.max(scores, axis=1, keepdims=True)
        weights = jnp.exp2((scores - peak) * scale2).astype(jnp.bfloat16)
        mixed = jnp.dot(weights, value_cols[...], preferred_element_type=jnp.float32)
        total = jnp.maximum(mixed[:, HD:2 * HD], 1.0)
        part = (mixed[:, 0:HD] / total).astype(jnp.bfloat16)
        spread = peak * scale2 + jnp.log2(total)
        at = 0
        for block, c in pairs:
            packed = jnp.zeros((8, HD), jnp.float32)
            for j in range(per_chunk):
                partials[block, c, :, pl.ds(j * HD, HD)] = part[at:at + rows]
                for i in range(groups):
                    slot = i * heads + c * per_chunk + j
                    packed = jnp.where(lane == slot, spread[at + 8 * i:at + 8 * i + 8], packed)
                at += rows
            spreads[block, c] = packed

    for c in range(0, CHUNKS, 2):
        compute([(me, c), (me, c + 1)])

    def gather_step(step, carry):
        b_right, b_left = place(-step), place(step)
        for position in range(CHUNKS):
            c_right, c_left = chunk_of(RIGHT, position), chunk_of(LEFT, position)
            for side, block, c in ((RIGHT, b_right, c_right), (LEFT, b_left, c_left)):
                gather_copy(side, step - 1, block, c).wait_recv()
                if position < half:
                    gather_copy(side, step, block, c).start()
                else:
                    @pl.when(step < reach - 1)
                    def _():
                        gather_copy(side, step, block, c).start()
            compute([(b_right, c_right), (b_left, c_left)])
            for side, block, c in ((RIGHT, b_right, c_right), (LEFT, b_left, c_left)):
                gather_copy(side, step - 1, block, c).wait_send()
        return carry

    lax.fori_loop(1, reach, gather_step, 0)
    far = place(reach)
    for position in range(half):
        pairs = [(far, chunk_of(side, position)) for side in (RIGHT, LEFT)]
        for side in (RIGHT, LEFT):
            gather_copy(side, reach - 1, far, pairs[side][1]).wait_recv()
        compute(pairs)

    def own_spread(block):
        spread = spreads[block, 0]
        for c in range(1, CHUNKS):
            spread = spread + spreads[block, c]
        row = block * rows + 8 * (lane // heads) + sublane
        sees = jnp.zeros((8, HD), jnp.int32)
        for begin, end, seen in bounds:
            sees = sees + jnp.where((row >= begin) & (row < end), seen, 0)
        return jnp.where((sees > 0) & (lane < groups * heads), spread, NEG)

    def along_rows(packed, c, j):
        slots = [i * heads + c * per_chunk + j for i in range(groups)]
        return jnp.concatenate(
            [jnp.broadcast_to(packed[:, s:s + 1], (8, HD)) for s in slots], axis=0
        )

    def pick(block, c, j):
        return partials[block, c, :, pl.ds(j * HD, HD)].astype(jnp.float32)

    def owner_at(side, step):
        return place(reach - step) if side == RIGHT else place(step - reach)

    far = inverse[place(reach)]
    for side in (RIGHT, LEFT):
        mine = (lane % heads) // per_chunk
        mine = mine < half if side == RIGHT else mine >= half
        leaving_spread[side, 0] = jnp.where(mine, own_spread(far), NEG)
        spread_copy(side, 0).start()
    for position in range(half):
        for side in (RIGHT, LEFT):
            c = chunk_of(side, position)
            leaving[side, 0, c] = partials[far, c]
            part_copy(side, 0, c).start()

    def merge_step(step, first):
        sources, keeps = [], []
        for side in (RIGHT, LEFT):
            source = inverse[owner_at(side, step)]
            spread_copy(side, step - 1).wait_recv()
            so_far, here = arrived_spread[side, step - 1], own_spread(source)
            top = jnp.maximum(so_far, here)
            both = top + jnp.log2(jnp.exp2(so_far - top) + jnp.exp2(here - top))
            leaving_spread[side, step] = both
            spread_copy(side, step).start()
            sources.append(source)
            keeps.append(jnp.exp2(so_far - both))
        for position in range(CHUNKS):
            for side in (RIGHT, LEFT):
                c = chunk_of(side, position)
                if first and position >= half:
                    leaving[side, step, c] = partials[sources[side], c]
                else:
                    part_copy(side, step - 1, c).wait_recv()
                    for j in range(per_chunk):
                        keep = along_rows(keeps[side], c, j)
                        before = arrived[side, step - 1, c, :, pl.ds(j * HD, HD)].astype(jnp.float32)
                        now = before * keep + pick(sources[side], c, j) * (1.0 - keep)
                        leaving[side, step, c, :, pl.ds(j * HD, HD)] = now.astype(jnp.bfloat16)
                part_copy(side, step, c).start()
        for side in (RIGHT, LEFT):
            spread_copy(side, step - 1).wait_send()
            for position in range(half if first else CHUNKS):
                part_copy(side, step - 1, chunk_of(side, position)).wait_send()

    merge_step(1, True)

    def merge_loop(step, carry):
        merge_step(step, False)
        return carry

    lax.fori_loop(2, reach, merge_loop, 0)

    source = inverse[me]
    for side in (RIGHT, LEFT):
        spread_copy(side, reach - 1).wait_recv()
    terms = [arrived_spread[RIGHT, reach - 1], arrived_spread[LEFT, reach - 1], own_spread(source)]
    top = jnp.maximum(jnp.maximum(terms[0], terms[1]), terms[2])
    terms = [jnp.exp2(term - top) for term in terms]
    total = terms[0] + terms[1] + terms[2]
    terms = [term / total for term in terms]
    stores = []
    for position in range(CHUNKS):
        c = position // 2 if position % 2 == 0 else CHUNKS - 1 - position // 2
        for side in (RIGHT, LEFT):
            part_copy(side, reach - 1, c).wait_recv()
        for j in range(per_chunk):
            full = pick(source, c, j) * along_rows(terms[2], c, j)
            for side in (RIGHT, LEFT):
                come = arrived[side, reach - 1, c, :, pl.ds(j * HD, HD)].astype(jnp.float32)
                full = full + come * along_rows(terms[side], c, j)
            merged[:, pl.ds(c * width + j * HD, HD)] = full.astype(jnp.bfloat16)
        columns = pl.ds(c * width, width)
        store = pltpu.make_async_copy(merged.at[:, columns], result.at[:, columns], store_sem.at[c])
        store.start()
        stores.append(store)
    for side in (RIGHT, LEFT):
        for position in range(half):
            gather_copy(side, reach - 1, me, chunk_of(side, position)).wait_send()
        spread_copy(side, reach - 1).wait_send()
        for c in range(CHUNKS):
            part_copy(side, reach - 1, c).wait_send()
    for store in stores:
        store.wait()


def per_device(queries, cached_keys, cached_values, turn_lengths, tile_map, prefix_len, owner_ids):
    n = lax.axis_size("ctx")
    rows, columns = queries.shape
    cache = cached_keys.shape[0]
    width = columns // CHUNKS
    reach = n // 2
    hbm = pl.BlockSpec(memory_space=pl.ANY)
    smem = pl.BlockSpec(memory_space=pltpu.SMEM)
    dma = pltpu.SemaphoreType.DMA
    return pl.pallas_call(
        kernel,
        out_shape=jax.ShapeDtypeStruct((rows, columns), jnp.bfloat16),
        in_specs=[hbm] * 3 + [smem] * 4,
        out_specs=hbm,
        scratch_shapes=[
            pltpu.VMEM((n, CHUNKS, rows, width), jnp.bfloat16),
            pltpu.VMEM((n, CHUNKS, rows, width), jnp.bfloat16),
            pltpu.VMEM((n, CHUNKS, 8, HD), jnp.float32),
            pltpu.VMEM((cache, HD), jnp.bfloat16),
            pltpu.VMEM((cache, HD), jnp.bfloat16),
            pltpu.VMEM((HD, cache), jnp.bfloat16),
            pltpu.VMEM((cache, 2 * HD), jnp.bfloat16),
            pltpu.SMEM((n,), jnp.int32),
            pltpu.VMEM((rows, columns), jnp.bfloat16),
            pltpu.VMEM((2, reach, CHUNKS, rows, width), jnp.bfloat16),
            pltpu.VMEM((2, reach, CHUNKS, rows, width), jnp.bfloat16),
            pltpu.VMEM((2, reach, 8, HD), jnp.float32),
            pltpu.VMEM((2, reach, 8, HD), jnp.float32),
            dma((CHUNKS + 2,)),
            dma((2, reach, CHUNKS)),
            dma((2, reach, CHUNKS)),
            dma((2, reach, CHUNKS)),
            dma((2, reach, CHUNKS)),
            dma((2, reach)),
            dma((2, reach)),
            dma((CHUNKS,)),
        ],
        compiler_params=pltpu.CompilerParams(
            collective_id=0, has_side_effects=True, vmem_limit_bytes=48 * 1024 * 1024
        ),
        cost_estimate=pl.CostEstimate(
            flops=4 * n * rows * columns * cache, bytes_accessed=1 << 20, transcendentals=n * rows * columns * cache // HD
        ),
    )(queries, cached_keys, cached_values, turn_lengths, tile_map, prefix_len, owner_ids)


def solution(mesh):
    return jax.shard_map(
        per_device,
        mesh=mesh,
        in_specs=(
            P(("pack", "ctx"), "head"),
            P(("pack", "ctx"), "head"),
            P(("pack", "ctx"), "head"),
            P("pack"),
            P("pack", None),
            P("pack"),
            P("pack"),
        ),
        out_specs=P(("pack", "ctx"), "head"),
        check_vma=False,
    )
```

```python
import math

import jax
import jax.numpy as jnp
from jax import lax
from jax.experimental import pallas as pl
from jax.experimental.pallas import tpu as pltpu
from jax.sharding import PartitionSpec as P

HD = 128
NEG = -1e30
MESH = pl.DeviceIdType.MESH
CHUNKS = 4
HALF = CHUNKS // 2
RIGHT, LEFT = 0, 1
SIDES = (RIGHT, LEFT)
KV_PIECES = 4
COUNT_ROWS = 16


def kernel(
    queries, cached_keys, cached_values, turn_lengths_in, tile_map_in, prefix_len_in, owner_ids_in,
    result,
    turn_lengths, tile_map, prefix_len, owner_ids, inverse,
    others, blocks, partials, spreads, keys, values, key_rows, value_cols, merged,
    arrived, leaving, arrived_spread, leaving_spread,
    load_sem, table_sem, kv_load, kv_send, kv_recv, gather_send, gather_recv,
    part_send, part_recv, spread_send, spread_recv, store_sem,
):
    n, _, rows, width = blocks.shape
    per_chunk = width // HD
    lanes = per_chunk * rows
    cache = keys.shape[1]
    piece = cache // KV_PIECES
    turns = turn_lengths.shape[0]
    steps = n // 4
    scale2 = HD ** (-0.5) * math.log2(math.e)
    me = lax.axis_index("ctx")
    core = lax.rem(lax.axis_index("pack"), 2)
    parity = lax.rem(me + core, 2)

    def place(offset):
        return lax.rem(me + offset + n, n)

    partner = place(1 - 2 * parity)

    def device(index):
        return {"ctx": index}

    def ahead(side, by):
        return place(by) if side == RIGHT else place(-by)

    def columns(c):
        return pl.ds(pl.multiple_of(c * width, width), width)

    own_loads = [
        pltpu.make_async_copy(
            queries.at[:, columns(HALF * parity + u)], blocks.at[me, u], load_sem.at[u]
        )
        for u in range(HALF)
    ]
    other_loads = [
        pltpu.make_async_copy(
            queries.at[:, columns(HALF * (1 - parity) + u)], others.at[u], load_sem.at[HALF + u]
        )
        for u in range(HALF)
    ]
    kv_loads = [
        pltpu.make_async_copy(cached_keys, keys.at[0], kv_load.at[0]),
        pltpu.make_async_copy(cached_values, values.at[0], kv_load.at[1]),
    ]
    tables = [
        pltpu.make_async_copy(source, target, table_sem.at[i])
        for i, (source, target) in enumerate(
            (
                (turn_lengths_in, turn_lengths),
                (tile_map_in, tile_map),
                (prefix_len_in, prefix_len),
                (owner_ids_in, owner_ids),
            )
        )
    ]
    for load in own_loads + other_loads + kv_loads + tables:
        load.start()

    barrier = pltpu.get_barrier_semaphore()
    for side in SIDES:
        for by in (1, 2):
            pl.semaphore_signal(
                barrier, inc=1, device_id=device(ahead(side, by)), device_id_type=MESH
            )
    pl.semaphore_wait(barrier, 4)

    def remote(source, target, send_sem, recv_sem, index):
        return pltpu.make_async_remote_copy(
            src_ref=source, dst_ref=target, send_sem=send_sem, recv_sem=recv_sem,
            device_id=device(index), device_id_type=MESH,
        )

    def gather_copy(side, step, kind, u, block, own_other=False):
        return remote(
            others.at[u] if own_other else blocks.at[block, u],
            blocks.at[block, u],
            gather_send.at[side, step, kind, u],
            gather_recv.at[side, step, kind, u],
            ahead(side, 1 if own_other else 2),
        )

    def kv_copy(which, p):
        source, target = ((cached_keys, keys), (cached_values, values))[which]
        part = pl.ds(p * piece, piece)
        return remote(
            source.at[part], target.at[1, part], kv_send.at[which, p], kv_recv.at[which, p], partner
        )

    def order(position):
        return (position % 2, position // 2) if isinstance(position, int) else (lax.rem(position, 2), position // 2)

    def goes_on(side, kind, u, step, last):
        return (step < last) | ((step == last) & ((kind == 1) | (u == side)))

    for load in own_loads + other_loads:
        load.wait()
    for u in range(HALF):
        for kind in range(2):
            for side in SIDES:
                gather_copy(side, 0, kind, u, me, own_other=kind == 1).start()
        if u == HALF - 1:
            for which in range(2):
                for p in range(KV_PIECES):
                    kv_copy(which, p).start()

    for table in tables:
        table.wait()
    for owner in range(n):
        source = jnp.int32(0)
        for b in range(n):
            source = jnp.maximum(source, jnp.where(owner_ids[b] == owner, b, 0))
        inverse[owner] = source
    shards = (me, partner)
    bounds = []
    begin = jnp.int32(0)
    for t in range(turns):
        end = begin + turn_lengths[t]
        bounds.append((begin, end, tile_map[t, me], tile_map[t, partner]))
        begin = end

    def prepare(s):
        limit = prefix_len[shards[s]]
        live = lax.broadcasted_iota(jnp.int32, (cache, HD), 0) < limit
        key_all = keys[s].astype(jnp.float32) * scale2
        key_all = jnp.where(live, key_all, jnp.broadcast_to(key_all[0:1, :], (cache, HD)))
        high = key_all.astype(jnp.bfloat16)
        key_rows[s, :, 0:HD] = high
        key_rows[s, :, HD:2 * HD] = (key_all - high.astype(jnp.float32)).astype(jnp.bfloat16)
        value_all = jnp.where(live, values[s].astype(jnp.float32), 0.0)
        value_cols[s, 0:HD, :] = value_all.T.astype(jnp.bfloat16)
        counted = lax.broadcasted_iota(jnp.int32, (COUNT_ROWS, cache), 1) < limit
        value_cols[s, HD:HD + COUNT_ROWS, :] = jnp.where(counted, 1.0, 0.0).astype(jnp.bfloat16)

    lane = lax.broadcasted_iota(jnp.int32, (2, lanes), 1)
    even_row = lax.broadcasted_iota(jnp.int32, (2, lanes), 0) == 0


    def score(s, pairs):
        query = jnp.concatenate(
            [
                blocks[block, u, :, pl.ds(j * HD, HD)]
                for block, u in pairs
                for j in range(per_chunk)
            ],
            axis=0,
        )
        query = jnp.concatenate([query, query], axis=1)
        scores = lax.dot_general(
            key_rows[s], query, (((1,), (1,)), ((), ())), preferred_element_type=jnp.float32
        )
        peak = jnp.max(scores.reshape(cache // 32, 32, scores.shape[1]), axis=0)
        return scores, jnp.max(peak, axis=0, keepdims=True)

    def absorb(s, pairs, scores, peak):
        weights = jnp.exp2(scores - peak).astype(jnp.bfloat16)
        mixed = jnp.dot(value_cols[s], weights, preferred_element_type=jnp.float32)
        total = jnp.maximum(mixed[HD:HD + 1, :], 1.0)
        part = (mixed[0:HD, :] * (1.0 / total)).astype(jnp.bfloat16)
        spread = peak + jnp.log2(total)
        for i, (block, u) in enumerate(pairs):
            partials[s, block, u] = part[:, i * lanes:(i + 1) * lanes]
            spreads[s, block, u] = jnp.broadcast_to(
                spread[:, i * lanes:(i + 1) * lanes], (2, lanes)
            )

    def compute(*units):
        ahead_of = score(*units[0])
        for i, unit in enumerate(units):
            now = ahead_of
            if i + 1 < len(units):
                ahead_of = score(*units[i + 1])
            absorb(*unit, *now)

    def block_at(side, step, kind):
        return place(kind - 2 * step) if side == RIGHT else place(2 * step - kind)

    def pairs_at(step, position):
        kind, u = order(position)
        return [(block_at(side, step, kind), u) for side in SIDES]

    def arrive(step, position, sides=SIDES):
        kind, u = order(position)
        for side in sides:
            block = block_at(side, step, kind)
            gather_copy(side, step - 1, kind, u, block).wait_recv()
            if isinstance(step, int) and step == steps:
                continue

            @pl.when(goes_on(side, kind, u, step, steps - 1))
            def _():
                gather_copy(side, step, kind, u, block).start()

    def sent(step, position):
        kind, u = order(position)
        for side in SIDES:
            gather_copy(side, step, kind, u, me).wait_send()

    own_pairs = [(me, 0), (me, 1)]
    for load in kv_loads:
        load.wait()
    prepare(0)
    compute((0, own_pairs))

    def early_step(it, carry):
        step, position = it // CHUNKS, lax.rem(it, CHUNKS)
        arrive(step, position)
        compute((0, pairs_at(step, position)))
        return carry

    lax.fori_loop(CHUNKS, 3 * CHUNKS, early_step, 0)
    for which in range(2):
        for p in range(KV_PIECES):
            kv_copy(which, p).wait_recv()
    prepare(1)
    compute((1, own_pairs))

    def late_step(position, carry):
        arrive(3, position)
        compute(
            (0, pairs_at(3, position)), *[(1, pairs_at(step, position)) for step in range(1, 4)]
        )
        for step in range(1, 4):
            sent(step - 1, position)
        return carry

    lax.fori_loop(0, CHUNKS, late_step, 0)

    def last_step(u):
        units = []
        for kind in range(2):
            sides = SIDES if kind == 1 else (u,)
            arrive(steps, 2 * u + kind, sides)
            pairs = [(block_at(side, steps, kind), u) for side in sides]
            units = units + [(0, pairs), (1, pairs)]
        compute(*units)

    def own_spread(s, even, odd, u):
        spread = jnp.where(even_row, spreads[s, even, u], spreads[s, odd, u])
        row = jnp.where(even_row, even, odd) * rows + lax.rem(lane, rows)
        sees = jnp.zeros((2, lanes), jnp.int32)
        for bound in bounds:
            sees = sees + jnp.where((row >= bound[0]) & (row < bound[1]), bound[2 + s], 0)
        return jnp.where(sees > 0, spread, NEG)

    def part_copy(side, step, kind, u):
        return remote(
            leaving.at[side, step, kind, u],
            arrived.at[side, step, kind, u],
            part_send.at[side, step, kind, u],
            part_recv.at[side, step, kind, u],
            ahead(side, 1 if step == steps - 1 and kind == 1 else 2),
        )

    def spread_copy(side, step, u, kind=0):
        to = step + 1 if kind == 1 else step
        return remote(
            leaving_spread.at[side, step, u],
            arrived_spread.at[side, to, u],
            spread_send.at[side, to, u],
            spread_recv.at[side, to, u],
            ahead(side, 1 if kind == 1 else 2),
        )

    def weights_of(terms):
        top = terms[0]
        for term in terms[1:]:
            top = jnp.maximum(top, term)
        terms = [jnp.exp2(term - top) for term in terms]
        total = terms[0]
        for term in terms[1:]:
            total = total + term
        return [term / total for term in terms], top + jnp.log2(total)

    def mix(kind, sources):
        full = None
        for weight, term in sources:
            term = term.astype(jnp.float32) * weight[kind:kind + 1, :]
            full = term if full is None else full + term
        return full

    def starts(side, kind, u, step):
        return step == 0 or (step == 1 and kind == 0 and u != side)

    def merge_step(step, u):
        for side in SIDES:
            far = 2 * (steps - step)
            blocks_of = [inverse[ahead(side, far)], inverse[ahead(side, far - 1)]]
            terms = [own_spread(s, *blocks_of, u) for s in range(2)]
            if step == 0:
                if u != side:
                    terms = [jnp.where(even_row, NEG, term) for term in terms]
            else:
                spread_copy(side, step - 1, u).wait_recv()
                terms.append(arrived_spread[side, step - 1, u])
            weights, spread = weights_of(terms)
            leaving_spread[side, step, u] = spread
            spread_copy(side, step, u).start()
            if step == steps - 1:
                spread_copy(side, step, u, 1).start()
            for kind in range(2):
                if step == 0 and kind == 0 and u != side:
                    continue
                come = [(weights[s], partials[s, blocks_of[kind], u]) for s in range(2)]
                if not starts(side, kind, u, step):
                    part_copy(side, step - 1, kind, u).wait_recv()
                    come.append((weights[2], arrived[side, step - 1, kind, u]))
                leaving[side, step, kind, u] = mix(kind, come).astype(jnp.bfloat16)
                part_copy(side, step, kind, u).start()

    for u in range(HALF):
        last_step(u)
        merge_step(0, u)
    for step in range(1, steps):
        for u in range(HALF):
            merge_step(step, u)

    source = inverse[me]
    stores = []
    for u in range(HALF):
        for side in SIDES:
            spread_copy(side, steps - 1, u).wait_recv()
            spread_copy(side, steps - 1, u, 1).wait_recv()
        own_weights, _ = weights_of(
            [own_spread(s, source, source, u) for s in range(2)]
            + [arrived_spread[side, steps - 1, u] for side in SIDES]
        )
        other_weights, _ = weights_of([arrived_spread[side, steps, u] for side in SIDES])
        for kind in range(2):
            for side in SIDES:
                part_copy(side, steps - 1, kind, u).wait_recv()
            come = [arrived[side, steps - 1, kind, u] for side in SIDES]
            if kind == 0:
                come = [partials[s, source, u] for s in range(2)] + come
            share = own_weights if kind == 0 else other_weights
            full = mix(kind, zip(share, come)).T.astype(jnp.bfloat16)
            c = HALF * (parity if kind == 0 else 1 - parity) + u
            for j in range(per_chunk):
                merged[c, :, pl.ds(j * HD, HD)] = full[j * rows:(j + 1) * rows]
            store = pltpu.make_async_copy(
                merged.at[c], result.at[:, columns(c)], store_sem.at[2 * u + kind]
            )
            store.start()
            stores.append(store)

    for side in SIDES:
        for u in range(HALF):
            for kind in range(2):
                if goes_on(side, kind, u, steps - 1, steps - 1):
                    gather_copy(side, steps - 1, kind, u, me).wait_send()
                for step in range(steps):
                    if step or kind == 1 or u == side:
                        part_copy(side, step, kind, u).wait_send()
            for step in range(steps):
                spread_copy(side, step, u).wait_send()
            spread_copy(side, steps - 1, u, 1).wait_send()
    for which in range(2):
        for p in range(KV_PIECES):
            kv_copy(which, p).wait_send()
    for store in stores:
        store.wait()


def per_device(queries, cached_keys, cached_values, turn_lengths, tile_map, prefix_len, owner_ids):
    n = lax.axis_size("ctx")
    rows, columns = queries.shape
    cache = cached_keys.shape[0]
    width = columns // CHUNKS
    steps = n // 4
    lanes = rows * width // HD
    hbm = pl.BlockSpec(memory_space=pl.ANY)
    dma = pltpu.SemaphoreType.DMA
    tables = (turn_lengths, tile_map, prefix_len, owner_ids)
    return pl.pallas_call(
        kernel,
        out_shape=jax.ShapeDtypeStruct((rows, columns), jnp.bfloat16),
        in_specs=[hbm] * 7,
        out_specs=hbm,
        scratch_shapes=[pltpu.SMEM(table.shape, jnp.int32) for table in tables]
        + [
            pltpu.SMEM((n,), jnp.int32),
            pltpu.VMEM((HALF, rows, width), jnp.bfloat16),
            pltpu.VMEM((n, HALF, rows, width), jnp.bfloat16),
            pltpu.VMEM((2, n, HALF, HD, lanes), jnp.bfloat16),
            pltpu.VMEM((2, n, HALF, 2, lanes), jnp.float32),
            pltpu.VMEM((2, cache, HD), jnp.bfloat16),
            pltpu.VMEM((2, cache, HD), jnp.bfloat16),
            pltpu.VMEM((2, cache, 2 * HD), jnp.bfloat16),
            pltpu.VMEM((2, HD + COUNT_ROWS, cache), jnp.bfloat16),
            pltpu.VMEM((CHUNKS, rows, width), jnp.bfloat16),
            pltpu.VMEM((2, steps, 2, HALF, HD, lanes), jnp.bfloat16),
            pltpu.VMEM((2, steps, 2, HALF, HD, lanes), jnp.bfloat16),
            pltpu.VMEM((2, steps + 1, HALF, 2, lanes), jnp.float32),
            pltpu.VMEM((2, steps, HALF, 2, lanes), jnp.float32),
            dma((CHUNKS,)),
            dma((len(tables),)),
            dma((2,)),
            dma((2, KV_PIECES)),
            dma((2, KV_PIECES)),
            dma((2, steps, 2, HALF)),
            dma((2, steps, 2, HALF)),
            dma((2, steps, 2, HALF)),
            dma((2, steps, 2, HALF)),
            dma((2, steps + 1, HALF)),
            dma((2, steps + 1, HALF)),
            dma((CHUNKS,)),
        ],
        compiler_params=pltpu.CompilerParams(
            collective_id=0, has_side_effects=True, vmem_limit_bytes=VMEM_BYTES
        ),
        cost_estimate=pl.CostEstimate(
            flops=4 * n * rows * columns * cache,
            bytes_accessed=1 << 20,
            transcendentals=n * rows * columns * cache // HD,
        ),
    )(queries, cached_keys, cached_values, *tables)


VMEM_BYTES = 62 * 1024 * 1024


def solution(mesh):
    return jax.shard_map(
        per_device,
        mesh=mesh,
        in_specs=(
            P(("pack", "ctx"), "head"),
            P(("pack", "ctx"), "head"),
            P(("pack", "ctx"), "head"),
            P("pack"),
            P("pack", None),
            P("pack"),
            P("pack"),
        ),
        out_specs=P(("pack", "ctx"), "head"),
        check_vma=False,
    )
```

```python
import math

import jax
import jax.numpy as jnp
from jax import lax
from jax.experimental import pallas as pl
from jax.experimental.pallas import tpu as pltpu
from jax.sharding import PartitionSpec as P

HD = 128
NEG = -1e30
MESH = pl.DeviceIdType.MESH
CHUNKS = 4
HALF = CHUNKS // 2
RIGHT, LEFT = 0, 1
SIDES = (RIGHT, LEFT)
KV_PIECES = 4
COUNT_ROWS = 16


def kernel(
    queries, cached_keys, cached_values, turn_lengths_in, tile_map_in, prefix_len_in, owner_ids_in,
    result,
    turn_lengths, tile_map, prefix_len, owner_ids, inverse,
    others, blocks, partials, spreads, keys, values, key_rows, value_cols,
    arrived, leaving, arrived_spread, leaving_spread,
    load_sem, table_sem, kv_load, kv_send, kv_recv, gather_send, gather_recv,
    part_send, part_recv, spread_send, spread_recv,
):
    n, _, rows, width = blocks.shape
    per_chunk = width // HD
    lanes = per_chunk * rows
    cache = keys.shape[1]
    piece = cache // KV_PIECES
    turns = turn_lengths.shape[0]
    steps = n // 4
    scale2 = HD ** (-0.5) * math.log2(math.e)
    me = lax.axis_index("ctx")
    core = lax.rem(lax.axis_index("pack"), 2)
    parity = lax.rem(me + core, 2)

    def place(offset):
        return lax.rem(me + offset + n, n)

    partner = place(1 - 2 * parity)

    def device(index):
        return {"ctx": index}

    def ahead(side, by):
        return place(by) if side == RIGHT else place(-by)

    def columns(c):
        return pl.ds(pl.multiple_of(c * width, width), width)

    own_loads = [
        pltpu.make_async_copy(
            queries.at[:, columns(HALF * parity + u)], blocks.at[me, u], load_sem.at[u]
        )
        for u in range(HALF)
    ]
    other_loads = [
        pltpu.make_async_copy(
            queries.at[:, columns(HALF * (1 - parity) + u)], others.at[u], load_sem.at[HALF + u]
        )
        for u in range(HALF)
    ]
    kv_loads = [
        pltpu.make_async_copy(cached_keys, keys.at[0], kv_load.at[0]),
        pltpu.make_async_copy(cached_values, values.at[0], kv_load.at[1]),
    ]
    tables = [
        pltpu.make_async_copy(source, target, table_sem.at[i])
        for i, (source, target) in enumerate(
            (
                (turn_lengths_in, turn_lengths),
                (tile_map_in, tile_map),
                (prefix_len_in, prefix_len),
                (owner_ids_in, owner_ids),
            )
        )
    ]
    for load in own_loads + other_loads + kv_loads + tables:
        load.start()

    barrier = pltpu.get_barrier_semaphore()
    for side in SIDES:
        for by in (1, 2):
            pl.semaphore_signal(
                barrier, inc=1, device_id=device(ahead(side, by)), device_id_type=MESH
            )
    pl.semaphore_wait(barrier, 4)

    def remote(source, target, send_sem, recv_sem, index):
        return pltpu.make_async_remote_copy(
            src_ref=source, dst_ref=target, send_sem=send_sem, recv_sem=recv_sem,
            device_id=device(index), device_id_type=MESH,
        )

    def gather_copy(side, step, kind, u, block, own_other=False):
        return remote(
            others.at[u] if own_other else blocks.at[block, u],
            blocks.at[block, u],
            gather_send.at[side, step, kind, u],
            gather_recv.at[side, step, kind, u],
            ahead(side, 1 if own_other else 2),
        )

    def kv_copy(which, p):
        source, target = ((cached_keys, keys), (cached_values, values))[which]
        part = pl.ds(p * piece, piece)
        return remote(
            source.at[part], target.at[1, part], kv_send.at[which, p], kv_recv.at[which, p], partner
        )

    def order(position):
        return (position % 2, position // 2) if isinstance(position, int) else (lax.rem(position, 2), position // 2)

    def goes_on(side, kind, u, step, last):
        return (step < last) | ((step == last) & ((kind == 1) | (u == side)))

    for load in own_loads + other_loads:
        load.wait()
    for u in range(HALF):
        for kind in range(2):
            for side in SIDES:
                gather_copy(side, 0, kind, u, me, own_other=kind == 1).start()
        if u == HALF - 1:
            for which in range(2):
                for p in range(KV_PIECES):
                    kv_copy(which, p).start()

    for table in tables:
        table.wait()
    for owner in range(n):
        source = jnp.int32(0)
        for b in range(n):
            source = jnp.maximum(source, jnp.where(owner_ids[b] == owner, b, 0))
        inverse[owner] = source
    shards = (me, partner)
    bounds = []
    begin = jnp.int32(0)
    for t in range(turns):
        end = begin + turn_lengths[t]
        bounds.append((begin, end, tile_map[t, me], tile_map[t, partner]))
        begin = end

    def prepare(s):
        limit = prefix_len[shards[s]]
        live = lax.broadcasted_iota(jnp.int32, (cache, HD), 0) < limit
        key_all = keys[s].astype(jnp.float32) * scale2
        key_all = jnp.where(live, key_all, jnp.broadcast_to(key_all[0:1, :], (cache, HD)))
        high = key_all.astype(jnp.bfloat16)
        key_rows[s, :, 0:HD] = high
        key_rows[s, :, HD:2 * HD] = (key_all - high.astype(jnp.float32)).astype(jnp.bfloat16)
        value_all = jnp.where(live, values[s].astype(jnp.float32), 0.0)
        value_cols[s, 0:HD, :] = value_all.T.astype(jnp.bfloat16)
        counted = lax.broadcasted_iota(jnp.int32, (COUNT_ROWS, cache), 1) < limit
        value_cols[s, HD:HD + COUNT_ROWS, :] = jnp.where(counted, 1.0, 0.0).astype(jnp.bfloat16)

    lane = lax.broadcasted_iota(jnp.int32, (2, lanes), 1)
    even_row = lax.broadcasted_iota(jnp.int32, (2, lanes), 0) == 0


    def score(s, pairs):
        query = jnp.concatenate(
            [
                blocks[block, u, :, pl.ds(j * HD, HD)]
                for block, u in pairs
                for j in range(per_chunk)
            ],
            axis=0,
        )
        query = jnp.concatenate([query, query], axis=1)
        scores = lax.dot_general(
            key_rows[s], query, (((1,), (1,)), ((), ())), preferred_element_type=jnp.float32
        )
        peak = jnp.max(scores.reshape(cache // 32, 32, scores.shape[1]), axis=0)
        return scores, jnp.max(peak, axis=0, keepdims=True)

    def absorb(s, pairs, scores, peak):
        weights = jnp.exp2(scores - peak).astype(jnp.bfloat16)
        mixed = jnp.dot(value_cols[s], weights, preferred_element_type=jnp.float32)
        total = jnp.maximum(mixed[HD:HD + 1, :], 1.0)
        part = (mixed[0:HD, :] * (1.0 / total)).astype(jnp.bfloat16)
        spread = peak + jnp.log2(total)
        for i, (block, u) in enumerate(pairs):
            partials[s, block, u] = part[:, i * lanes:(i + 1) * lanes]
            spreads[s, block, u] = jnp.broadcast_to(
                spread[:, i * lanes:(i + 1) * lanes], (2, lanes)
            )

    def compute(*units):
        ahead_of = score(*units[0])
        for i, unit in enumerate(units):
            now = ahead_of
            if i + 1 < len(units):
                ahead_of = score(*units[i + 1])
            absorb(*unit, *now)

    def block_at(side, step, kind):
        return place(kind - 2 * step) if side == RIGHT else place(2 * step - kind)

    def pairs_at(step, position):
        kind, u = order(position)
        return [(block_at(side, step, kind), u) for side in SIDES]

    def arrive(step, position, sides=SIDES):
        kind, u = order(position)
        for side in sides:
            block = block_at(side, step, kind)
            gather_copy(side, step - 1, kind, u, block).wait_recv()
            if isinstance(step, int) and step == steps:
                continue

            @pl.when(goes_on(side, kind, u, step, steps - 1))
            def _():
                gather_copy(side, step, kind, u, block).start()

    def sent(step, position):
        kind, u = order(position)
        for side in SIDES:
            gather_copy(side, step, kind, u, me).wait_send()

    own_pairs = [(me, 0), (me, 1)]
    for load in kv_loads:
        load.wait()
    prepare(0)
    compute((0, own_pairs))

    def early_step(it, carry):
        step, position = it // CHUNKS, lax.rem(it, CHUNKS)
        arrive(step, position)
        compute((0, pairs_at(step, position)))
        return carry

    lax.fori_loop(CHUNKS, 3 * CHUNKS, early_step, 0)
    for which in range(2):
        for p in range(KV_PIECES):
            kv_copy(which, p).wait_recv()
    prepare(1)
    compute((1, own_pairs))

    def late_step(position, carry):
        arrive(3, position)
        compute(
            (0, pairs_at(3, position)), *[(1, pairs_at(step, position)) for step in range(1, 4)]
        )
        for step in range(1, 4):
            sent(step - 1, position)
        return carry

    lax.fori_loop(0, CHUNKS, late_step, 0)

    def last_step(u):
        units = []
        for kind in range(2):
            sides = SIDES if kind == 1 else (u,)
            arrive(steps, 2 * u + kind, sides)
            pairs = [(block_at(side, steps, kind), u) for side in sides]
            units = units + [(0, pairs), (1, pairs)]
        compute(*units)

    def own_spread(s, even, odd, u):
        spread = jnp.where(even_row, spreads[s, even, u], spreads[s, odd, u])
        row = jnp.where(even_row, even, odd) * rows + lax.rem(lane, rows)
        sees = jnp.zeros((2, lanes), jnp.int32)
        for bound in bounds:
            sees = sees + jnp.where((row >= bound[0]) & (row < bound[1]), bound[2 + s], 0)
        return jnp.where(sees > 0, spread, NEG)

    def part_copy(side, step, kind, u):
        return remote(
            leaving.at[side, step, kind, u],
            arrived.at[side, step, kind, u],
            part_send.at[side, step, kind, u],
            part_recv.at[side, step, kind, u],
            ahead(side, 1 if step == steps - 1 and kind == 1 else 2),
        )

    def spread_copy(side, step, u, kind=0):
        to = step + 1 if kind == 1 else step
        return remote(
            leaving_spread.at[side, step, u],
            arrived_spread.at[side, to, u],
            spread_send.at[side, to, u],
            spread_recv.at[side, to, u],
            ahead(side, 1 if kind == 1 else 2),
        )

    def weights_of(terms):
        top = terms[0]
        for term in terms[1:]:
            top = jnp.maximum(top, term)
        terms = [jnp.exp2(term - top) for term in terms]
        total = terms[0]
        for term in terms[1:]:
            total = total + term
        return [term / total for term in terms], top + jnp.log2(total)

    def mix(kind, sources):
        full = None
        for weight, term in sources:
            term = term.astype(jnp.float32) * weight[kind:kind + 1, :]
            full = term if full is None else full + term
        return full

    def starts(side, kind, u, step):
        return step == 0 or (step == 1 and kind == 0 and u != side)

    def merge_step(step, u):
        for side in SIDES:
            far = 2 * (steps - step)
            blocks_of = [inverse[ahead(side, far)], inverse[ahead(side, far - 1)]]
            terms = [own_spread(s, *blocks_of, u) for s in range(2)]
            if step == 0:
                if u != side:
                    terms = [jnp.where(even_row, NEG, term) for term in terms]
            else:
                spread_copy(side, step - 1, u).wait_recv()
                terms.append(arrived_spread[side, step - 1, u])
            weights, spread = weights_of(terms)
            leaving_spread[side, step, u] = spread
            spread_copy(side, step, u).start()
            if step == steps - 1:
                spread_copy(side, step, u, 1).start()
            for kind in range(2):
                if step == 0 and kind == 0 and u != side:
                    continue
                come = [(weights[s], partials[s, blocks_of[kind], u]) for s in range(2)]
                if not starts(side, kind, u, step):
                    part_copy(side, step - 1, kind, u).wait_recv()
                    come.append((weights[2], arrived[side, step - 1, kind, u]))
                leaving[side, step, kind, u] = mix(kind, come).astype(jnp.bfloat16)
                part_copy(side, step, kind, u).start()

    for u in range(HALF):
        last_step(u)
        merge_step(0, u)
    for step in range(1, steps):
        for u in range(HALF):
            merge_step(step, u)

    source = inverse[me]
    for u in range(HALF):
        for side in SIDES:
            spread_copy(side, steps - 1, u).wait_recv()
            spread_copy(side, steps - 1, u, 1).wait_recv()
        own_weights, _ = weights_of(
            [own_spread(s, source, source, u) for s in range(2)]
            + [arrived_spread[side, steps - 1, u] for side in SIDES]
        )
        other_weights, _ = weights_of([arrived_spread[side, steps, u] for side in SIDES])
        for kind in range(2):
            for side in SIDES:
                part_copy(side, steps - 1, kind, u).wait_recv()
            come = [arrived[side, steps - 1, kind, u] for side in SIDES]
            if kind == 0:
                come = [partials[s, source, u] for s in range(2)] + come
            share = own_weights if kind == 0 else other_weights
            full = mix(kind, zip(share, come)).T.astype(jnp.bfloat16)
            c = HALF * (parity if kind == 0 else 1 - parity) + u
            for j in range(per_chunk):
                at = pl.ds(pl.multiple_of(c * width + j * HD, HD), HD)
                result[:, at] = full[j * rows:(j + 1) * rows]

    for side in SIDES:
        for u in range(HALF):
            for kind in range(2):
                if goes_on(side, kind, u, steps - 1, steps - 1):
                    gather_copy(side, steps - 1, kind, u, me).wait_send()
                for step in range(steps):
                    if step or kind == 1 or u == side:
                        part_copy(side, step, kind, u).wait_send()
            for step in range(steps):
                spread_copy(side, step, u).wait_send()
            spread_copy(side, steps - 1, u, 1).wait_send()
    for which in range(2):
        for p in range(KV_PIECES):
            kv_copy(which, p).wait_send()


def per_device(queries, cached_keys, cached_values, turn_lengths, tile_map, prefix_len, owner_ids):
    n = lax.axis_size("ctx")
    rows, columns = queries.shape
    cache = cached_keys.shape[0]
    width = columns // CHUNKS
    steps = n // 4
    lanes = rows * width // HD
    hbm = pl.BlockSpec(memory_space=pl.ANY)
    dma = pltpu.SemaphoreType.DMA
    tables = (turn_lengths, tile_map, prefix_len, owner_ids)
    return pl.pallas_call(
        kernel,
        out_shape=pltpu.VMEM((rows, columns), jnp.bfloat16),
        in_specs=[hbm] * 7,
        out_specs=pl.BlockSpec(memory_space=pltpu.VMEM),
        scratch_shapes=[pltpu.SMEM(table.shape, jnp.int32) for table in tables]
        + [
            pltpu.SMEM((n,), jnp.int32),
            pltpu.VMEM((HALF, rows, width), jnp.bfloat16),
            pltpu.VMEM((n, HALF, rows, width), jnp.bfloat16),
            pltpu.VMEM((2, n, HALF, HD, lanes), jnp.bfloat16),
            pltpu.VMEM((2, n, HALF, 2, lanes), jnp.float32),
            pltpu.VMEM((2, cache, HD), jnp.bfloat16),
            pltpu.VMEM((2, cache, HD), jnp.bfloat16),
            pltpu.VMEM((2, cache, 2 * HD), jnp.bfloat16),
            pltpu.VMEM((2, HD + COUNT_ROWS, cache), jnp.bfloat16),
            pltpu.VMEM((2, steps, 2, HALF, HD, lanes), jnp.bfloat16),
            pltpu.VMEM((2, steps, 2, HALF, HD, lanes), jnp.bfloat16),
            pltpu.VMEM((2, steps + 1, HALF, 2, lanes), jnp.float32),
            pltpu.VMEM((2, steps, HALF, 2, lanes), jnp.float32),
            dma((CHUNKS,)),
            dma((len(tables),)),
            dma((2,)),
            dma((2, KV_PIECES)),
            dma((2, KV_PIECES)),
            dma((2, steps, 2, HALF)),
            dma((2, steps, 2, HALF)),
            dma((2, steps, 2, HALF)),
            dma((2, steps, 2, HALF)),
            dma((2, steps + 1, HALF)),
            dma((2, steps + 1, HALF)),
        ],
        compiler_params=pltpu.CompilerParams(
            collective_id=0, has_side_effects=True, vmem_limit_bytes=VMEM_BYTES
        ),
        cost_estimate=pl.CostEstimate(
            flops=4 * n * rows * columns * cache,
            bytes_accessed=1 << 20,
            transcendentals=n * rows * columns * cache // HD,
        ),
    )(*[pltpu.with_memory_space_constraint(x, pltpu.HBM) for x in (queries, cached_keys, cached_values, *tables)])


VMEM_BYTES = 48 * 1024 * 1024


def solution(mesh):
    return jax.shard_map(
        per_device,
        mesh=mesh,
        in_specs=(
            P(("pack", "ctx"), "head"),
            P(("pack", "ctx"), "head"),
            P(("pack", "ctx"), "head"),
            P("pack"),
            P("pack", None),
            P("pack"),
            P("pack"),
        ),
        out_specs=P(("pack", "ctx"), "head"),
        check_vma=False,
    )
```

```python
import math

import jax
import jax.numpy as jnp
from jax import lax
from jax.experimental import pallas as pl
from jax.experimental.pallas import tpu as pltpu
from jax.sharding import PartitionSpec as P

HD = 128
NEG = -1e30
MESH = pl.DeviceIdType.MESH
CHUNKS = 4
HALF = CHUNKS // 2
RIGHT, LEFT = 0, 1
SIDES = (RIGHT, LEFT)
KV_PIECES = 4
COUNT_ROWS = 16


def kernel(
    queries, cached_keys, cached_values, turn_lengths_in, tile_map_in, prefix_len_in, owner_ids_in,
    result,
    turn_lengths, tile_map, prefix_len, owner_ids, inverse,
    others, blocks, partials, spreads, keys, values, key_rows, value_cols,
    arrived, leaving, arrived_spread, leaving_spread,
    load_sem, table_sem, kv_load, kv_send, kv_recv, gather_send, gather_recv,
    part_send, part_recv, spread_send, spread_recv,
):
    n, _, rows, width = blocks.shape
    per_chunk = width // HD
    lanes = per_chunk * rows
    cache = keys.shape[1]
    piece = cache // KV_PIECES
    turns = turn_lengths.shape[0]
    steps = n // 4
    scale2 = HD ** (-0.5) * math.log2(math.e)
    me = lax.axis_index("ctx")
    core = lax.rem(lax.axis_index("pack"), 2)
    parity = lax.rem(me + core, 2)

    def place(offset):
        return lax.rem(me + offset + n, n)

    partner = place(1 - 2 * parity)

    def device(index):
        return {"ctx": index}

    def ahead(side, by):
        return place(by) if side == RIGHT else place(-by)

    def columns(c):
        return pl.ds(pl.multiple_of(c * width, width), width)

    barrier = pltpu.get_barrier_semaphore()
    for side in SIDES:
        for by in (1, 2):
            pl.semaphore_signal(
                barrier, inc=1, device_id=device(ahead(side, by)), device_id_type=MESH
            )

    own_loads = [
        pltpu.make_async_copy(
            queries.at[:, columns(HALF * parity + u)], blocks.at[me, u], load_sem.at[u]
        )
        for u in range(HALF)
    ]
    other_loads = [
        pltpu.make_async_copy(
            queries.at[:, columns(HALF * (1 - parity) + u)], others.at[u], load_sem.at[HALF + u]
        )
        for u in range(HALF)
    ]
    kv_loads = [
        pltpu.make_async_copy(cached_keys, keys.at[0], kv_load.at[0]),
        pltpu.make_async_copy(cached_values, values.at[0], kv_load.at[1]),
    ]
    tables = [
        pltpu.make_async_copy(source, target, table_sem.at[i])
        for i, (source, target) in enumerate(
            (
                (turn_lengths_in, turn_lengths),
                (tile_map_in, tile_map),
                (prefix_len_in, prefix_len),
                (owner_ids_in, owner_ids),
            )
        )
    ]
    for load in own_loads + other_loads:
        load.start()

    pl.semaphore_wait(barrier, 4)

    def remote(source, target, send_sem, recv_sem, index):
        return pltpu.make_async_remote_copy(
            src_ref=source, dst_ref=target, send_sem=send_sem, recv_sem=recv_sem,
            device_id=device(index), device_id_type=MESH,
        )

    def gather_copy(side, step, kind, u, block, own_other=False):
        return remote(
            others.at[u] if own_other else blocks.at[block, u],
            blocks.at[block, u],
            gather_send.at[side, step, kind, u],
            gather_recv.at[side, step, kind, u],
            ahead(side, 1 if own_other else 2),
        )

    def kv_copy(which, p):
        source, target = ((cached_keys, keys), (cached_values, values))[which]
        part = pl.ds(p * piece, piece)
        return remote(
            source.at[part], target.at[1, part], kv_send.at[which, p], kv_recv.at[which, p], partner
        )

    def order(position):
        return (position % 2, position // 2) if isinstance(position, int) else (lax.rem(position, 2), position // 2)

    def goes_on(side, kind, u, step, last):
        return (step < last) | ((step == last) & ((kind == 1) | (u == side)))

    for load in own_loads + other_loads:
        load.wait()
    for u in range(HALF):
        for kind in range(2):
            for side in SIDES:
                gather_copy(side, 0, kind, u, me, own_other=kind == 1).start()
        if u == HALF - 1:
            for which in range(2):
                for p in range(KV_PIECES):
                    kv_copy(which, p).start()

    for load in kv_loads + tables:
        load.start()
    for table in tables:
        table.wait()
    for owner in range(n):
        source = jnp.int32(0)
        for b in range(n):
            source = jnp.maximum(source, jnp.where(owner_ids[b] == owner, b, 0))
        inverse[owner] = source
    shards = (me, partner)
    bounds = []
    begin = jnp.int32(0)
    for t in range(turns):
        end = begin + turn_lengths[t]
        bounds.append((begin, end, tile_map[t, me], tile_map[t, partner]))
        begin = end

    def prepare(s):
        limit = prefix_len[shards[s]]
        live = lax.broadcasted_iota(jnp.int32, (cache, HD), 0) < limit
        key_all = keys[s].astype(jnp.float32) * scale2
        key_all = jnp.where(live, key_all, jnp.broadcast_to(key_all[0:1, :], (cache, HD)))
        high = key_all.astype(jnp.bfloat16)
        key_rows[s, :, 0:HD] = high
        key_rows[s, :, HD:2 * HD] = (key_all - high.astype(jnp.float32)).astype(jnp.bfloat16)
        value_all = jnp.where(live, values[s].astype(jnp.float32), 0.0)
        value_cols[s, 0:HD, :] = value_all.T.astype(jnp.bfloat16)
        counted = lax.broadcasted_iota(jnp.int32, (COUNT_ROWS, cache), 1) < limit
        value_cols[s, HD:HD + COUNT_ROWS, :] = jnp.where(counted, 1.0, 0.0).astype(jnp.bfloat16)

    lane = lax.broadcasted_iota(jnp.int32, (2, lanes), 1)
    even_row = lax.broadcasted_iota(jnp.int32, (2, lanes), 0) == 0


    def score(s, pairs):
        query = jnp.concatenate(
            [
                blocks[block, u, :, pl.ds(j * HD, HD)]
                for block, u in pairs
                for j in range(per_chunk)
            ],
            axis=0,
        )
        query = jnp.concatenate([query, query], axis=1)
        scores = lax.dot_general(
            key_rows[s], query, (((1,), (1,)), ((), ())), preferred_element_type=jnp.float32
        )
        peak = jnp.max(scores.reshape(cache // 32, 32, scores.shape[1]), axis=0)
        return scores, jnp.max(peak, axis=0, keepdims=True)

    def absorb(s, pairs, scores, peak):
        weights = jnp.exp2(scores - peak).astype(jnp.bfloat16)
        mixed = jnp.dot(value_cols[s], weights, preferred_element_type=jnp.float32)
        total = jnp.maximum(mixed[HD:HD + 1, :], 1.0)
        part = (mixed[0:HD, :] * (1.0 / total)).astype(jnp.bfloat16)
        spread = peak + jnp.log2(total)
        for i, (block, u) in enumerate(pairs):
            partials[s, block, u] = part[:, i * lanes:(i + 1) * lanes]
            spreads[s, block, u] = jnp.broadcast_to(
                spread[:, i * lanes:(i + 1) * lanes], (2, lanes)
            )

    def compute(*units):
        ahead_of = score(*units[0])
        for i, unit in enumerate(units):
            now = ahead_of
            if i + 1 < len(units):
                ahead_of = score(*units[i + 1])
            absorb(*unit, *now)

    def block_at(side, step, kind):
        return place(kind - 2 * step) if side == RIGHT else place(2 * step - kind)

    def pairs_at(step, position):
        kind, u = order(position)
        return [(block_at(side, step, kind), u) for side in SIDES]

    def arrive(step, position, sides=SIDES):
        kind, u = order(position)
        for side in sides:
            block = block_at(side, step, kind)
            gather_copy(side, step - 1, kind, u, block).wait_recv()
            if isinstance(step, int) and step == steps:
                continue

            @pl.when(goes_on(side, kind, u, step, steps - 1))
            def _():
                gather_copy(side, step, kind, u, block).start()

    def sent(step, position):
        kind, u = order(position)
        for side in SIDES:
            gather_copy(side, step, kind, u, me).wait_send()

    own_pairs = [(me, 0), (me, 1)]
    for load in kv_loads:
        load.wait()
    prepare(0)
    compute((0, own_pairs))

    def early_step(it, carry):
        step, position = it // CHUNKS, lax.rem(it, CHUNKS)
        arrive(step, position)
        compute((0, pairs_at(step, position)))
        return carry

    lax.fori_loop(CHUNKS, 3 * CHUNKS, early_step, 0)
    for which in range(2):
        for p in range(KV_PIECES):
            kv_copy(which, p).wait_recv()
    prepare(1)
    compute((1, own_pairs))

    def late_step(position, carry):
        arrive(3, position)
        compute(
            (0, pairs_at(3, position)), *[(1, pairs_at(step, position)) for step in range(1, 4)]
        )
        for step in range(1, 4):
            sent(step - 1, position)
        return carry

    lax.fori_loop(0, CHUNKS, late_step, 0)

    def last_step(u):
        units = []
        for kind in range(2):
            sides = SIDES if kind == 1 else (u,)
            arrive(steps, 2 * u + kind, sides)
            pairs = [(block_at(side, steps, kind), u) for side in sides]
            units = units + [(0, pairs), (1, pairs)]
        compute(*units)

    def own_spread(s, even, odd, u):
        spread = jnp.where(even_row, spreads[s, even, u], spreads[s, odd, u])
        row = jnp.where(even_row, even, odd) * rows + lax.rem(lane, rows)
        sees = jnp.zeros((2, lanes), jnp.int32)
        for bound in bounds:
            sees = sees + jnp.where((row >= bound[0]) & (row < bound[1]), bound[2 + s], 0)
        return jnp.where(sees > 0, spread, NEG)

    def part_copy(side, step, kind, u):
        return remote(
            leaving.at[side, step, kind, u],
            arrived.at[side, step, kind, u],
            part_send.at[side, step, kind, u],
            part_recv.at[side, step, kind, u],
            ahead(side, 1 if step == steps - 1 and kind == 1 else 2),
        )

    def spread_copy(side, step, u, kind=0):
        to = step + 1 if kind == 1 else step
        return remote(
            leaving_spread.at[side, step, u],
            arrived_spread.at[side, to, u],
            spread_send.at[side, to, u],
            spread_recv.at[side, to, u],
            ahead(side, 1 if kind == 1 else 2),
        )

    def weights_of(terms):
        top = terms[0]
        for term in terms[1:]:
            top = jnp.maximum(top, term)
        terms = [jnp.exp2(term - top) for term in terms]
        total = terms[0]
        for term in terms[1:]:
            total = total + term
        return [term / total for term in terms], top + jnp.log2(total)

    def mix(kind, sources):
        full = None
        for weight, term in sources:
            term = term.astype(jnp.float32) * weight[kind:kind + 1, :]
            full = term if full is None else full + term
        return full

    def starts(side, kind, u, step):
        return step == 0 or (step == 1 and kind == 0 and u != side)

    def merge_step(step, u):
        blocks_at, shares = [], []
        for side in SIDES:
            far = 2 * (steps - step)
            blocks_of = [inverse[ahead(side, far)], inverse[ahead(side, far - 1)]]
            terms = [own_spread(s, *blocks_of, u) for s in range(2)]
            if step == 0:
                if u != side:
                    terms = [jnp.where(even_row, NEG, term) for term in terms]
            else:
                spread_copy(side, step - 1, u).wait_recv()
                terms.append(arrived_spread[side, step - 1, u])
            weights, spread = weights_of(terms)
            leaving_spread[side, step, u] = spread
            spread_copy(side, step, u).start()
            if step == steps - 1:
                spread_copy(side, step, u, 1).start()
            blocks_at.append(blocks_of)
            shares.append(weights)
        for kind in range(2):
            for side in SIDES:
                if step == 0 and kind == 0 and u != side:
                    continue
                come = [(shares[side][s], partials[s, blocks_at[side][kind], u]) for s in range(2)]
                if not starts(side, kind, u, step):
                    part_copy(side, step - 1, kind, u).wait_recv()
                    come.append((shares[side][2], arrived[side, step - 1, kind, u]))
                leaving[side, step, kind, u] = mix(kind, come).astype(jnp.bfloat16)
                part_copy(side, step, kind, u).start()

    for u in range(HALF):
        last_step(u)
        merge_step(0, u)
    for step in range(1, steps):
        for u in range(HALF):
            merge_step(step, u)

    def settle(merge_steps):
        for side in SIDES:
            for u in range(HALF):
                for step in merge_steps:
                    for kind in range(2):
                        if step or kind == 1 or u == side:
                            part_copy(side, step, kind, u).wait_send()
                    spread_copy(side, step, u).wait_send()
                    if step == steps - 1:
                        spread_copy(side, step, u, 1).wait_send()

    for side in SIDES:
        for u in range(HALF):
            for kind in range(2):
                if goes_on(side, kind, u, steps - 1, steps - 1):
                    gather_copy(side, steps - 1, kind, u, me).wait_send()
    for which in range(2):
        for p in range(KV_PIECES):
            kv_copy(which, p).wait_send()
    settle(range(steps - 1))

    source = inverse[me]
    for u in range(HALF):
        for side in SIDES:
            spread_copy(side, steps - 1, u).wait_recv()
            spread_copy(side, steps - 1, u, 1).wait_recv()
        own_weights, _ = weights_of(
            [own_spread(s, source, source, u) for s in range(2)]
            + [arrived_spread[side, steps - 1, u] for side in SIDES]
        )
        other_weights, _ = weights_of([arrived_spread[side, steps, u] for side in SIDES])
        for kind in range(2):
            for side in SIDES:
                part_copy(side, steps - 1, kind, u).wait_recv()
            come = [arrived[side, steps - 1, kind, u] for side in SIDES]
            if kind == 0:
                come = [partials[s, source, u] for s in range(2)] + come
            share = own_weights if kind == 0 else other_weights
            full = mix(kind, zip(share, come)).T.astype(jnp.bfloat16)
            c = HALF * (parity if kind == 0 else 1 - parity) + u
            for j in range(per_chunk):
                at = pl.ds(pl.multiple_of(c * width + j * HD, HD), HD)
                result[:, at] = full[j * rows:(j + 1) * rows]

    settle(range(steps - 1, steps))


def per_device(queries, cached_keys, cached_values, turn_lengths, tile_map, prefix_len, owner_ids):
    n = lax.axis_size("ctx")
    rows, columns = queries.shape
    cache = cached_keys.shape[0]
    width = columns // CHUNKS
    steps = n // 4
    lanes = rows * width // HD
    hbm = pl.BlockSpec(memory_space=pl.ANY)
    dma = pltpu.SemaphoreType.DMA
    tables = (turn_lengths, tile_map, prefix_len, owner_ids)
    return pl.pallas_call(
        kernel,
        out_shape=pltpu.VMEM((rows, columns), jnp.bfloat16),
        in_specs=[hbm] * 7,
        out_specs=pl.BlockSpec(memory_space=pltpu.VMEM),
        scratch_shapes=[pltpu.SMEM(table.shape, jnp.int32) for table in tables]
        + [
            pltpu.SMEM((n,), jnp.int32),
            pltpu.VMEM((HALF, rows, width), jnp.bfloat16),
            pltpu.VMEM((n, HALF, rows, width), jnp.bfloat16),
            pltpu.VMEM((2, n, HALF, HD, lanes), jnp.bfloat16),
            pltpu.VMEM((2, n, HALF, 2, lanes), jnp.float32),
            pltpu.VMEM((2, cache, HD), jnp.bfloat16),
            pltpu.VMEM((2, cache, HD), jnp.bfloat16),
            pltpu.VMEM((2, cache, 2 * HD), jnp.bfloat16),
            pltpu.VMEM((2, HD + COUNT_ROWS, cache), jnp.bfloat16),
            pltpu.VMEM((2, steps, 2, HALF, HD, lanes), jnp.bfloat16),
            pltpu.VMEM((2, steps, 2, HALF, HD, lanes), jnp.bfloat16),
            pltpu.VMEM((2, steps + 1, HALF, 2, lanes), jnp.float32),
            pltpu.VMEM((2, steps, HALF, 2, lanes), jnp.float32),
            dma((CHUNKS,)),
            dma((len(tables),)),
            dma((2,)),
            dma((2, KV_PIECES)),
            dma((2, KV_PIECES)),
            dma((2, steps, 2, HALF)),
            dma((2, steps, 2, HALF)),
            dma((2, steps, 2, HALF)),
            dma((2, steps, 2, HALF)),
            dma((2, steps + 1, HALF)),
            dma((2, steps + 1, HALF)),
        ],
        compiler_params=pltpu.CompilerParams(
            collective_id=0, has_side_effects=True, vmem_limit_bytes=VMEM_BYTES
        ),
        cost_estimate=pl.CostEstimate(
            flops=4 * n * rows * columns * cache,
            bytes_accessed=1 << 20,
            transcendentals=n * rows * columns * cache // HD,
        ),
    )(*[pltpu.with_memory_space_constraint(x, pltpu.HBM) for x in (queries, cached_keys, cached_values, *tables)])


VMEM_BYTES = 48 * 1024 * 1024


def solution(mesh):
    return jax.shard_map(
        per_device,
        mesh=mesh,
        in_specs=(
            P(("pack", "ctx"), "head"),
            P(("pack", "ctx"), "head"),
            P(("pack", "ctx"), "head"),
            P("pack"),
            P("pack", None),
            P("pack"),
            P("pack"),
        ),
        out_specs=P(("pack", "ctx"), "head"),
        check_vma=False,
    )
```

```python
import math

import jax
import jax.numpy as jnp
from jax import lax
from jax.experimental import pallas as pl
from jax.experimental.pallas import tpu as pltpu
from jax.sharding import PartitionSpec as P

HD = 128
NEG = -1e30
MESH = pl.DeviceIdType.MESH
CHUNKS = 4
HALF = CHUNKS // 2
RIGHT, LEFT = 0, 1
SIDES = (RIGHT, LEFT)
KV_PIECES = 2
COUNT_ROWS = 16


def kernel(
    queries, cached_keys, cached_values, turn_lengths_in, tile_map_in, prefix_len_in, owner_ids_in,
    result,
    turn_lengths, tile_map, prefix_len, owner_ids, inverse,
    others, blocks, partials, spreads, keys, values, key_rows, value_cols,
    arrived, leaving, arrived_spread, leaving_spread,
    load_sem, table_sem, kv_load, kv_send, kv_recv, gather_send, gather_recv,
    part_send, part_recv, spread_send, spread_recv,
):
    n, _, rows, width = blocks.shape
    per_chunk = width // HD
    lanes = per_chunk * rows
    cache = keys.shape[1]
    piece = cache // KV_PIECES
    turns = turn_lengths.shape[0]
    steps = n // 4
    scale2 = HD ** (-0.5) * math.log2(math.e)
    me = lax.axis_index("ctx")
    core = lax.rem(lax.axis_index("pack"), 2)
    parity = lax.rem(me + core, 2)

    def place(offset):
        return lax.rem(me + offset + n, n)

    partner = place(1 - 2 * parity)

    def device(index):
        return {"ctx": index}

    def ahead(side, by):
        return place(by) if side == RIGHT else place(-by)

    def columns(c):
        return pl.ds(pl.multiple_of(c * width, width), width)

    barrier = pltpu.get_barrier_semaphore()
    for side in SIDES:
        for by in (1, 2):
            pl.semaphore_signal(
                barrier, inc=1, device_id=device(ahead(side, by)), device_id_type=MESH
            )

    own_loads = [
        pltpu.make_async_copy(
            queries.at[:, columns(HALF * parity + u)], blocks.at[me, u], load_sem.at[u]
        )
        for u in range(HALF)
    ]
    other_loads = [
        pltpu.make_async_copy(
            queries.at[:, columns(HALF * (1 - parity) + u)], others.at[u], load_sem.at[HALF + u]
        )
        for u in range(HALF)
    ]
    kv_loads = [
        pltpu.make_async_copy(cached_keys, keys.at[0], kv_load.at[0]),
        pltpu.make_async_copy(cached_values, values.at[0], kv_load.at[1]),
    ]
    tables = [
        pltpu.make_async_copy(source, target, table_sem.at[i])
        for i, (source, target) in enumerate(
            (
                (turn_lengths_in, turn_lengths),
                (tile_map_in, tile_map),
                (prefix_len_in, prefix_len),
                (owner_ids_in, owner_ids),
            )
        )
    ]
    for load in own_loads + other_loads:
        load.start()

    pl.semaphore_wait(barrier, 4)

    def remote(source, target, send_sem, recv_sem, index):
        return pltpu.make_async_remote_copy(
            src_ref=source, dst_ref=target, send_sem=send_sem, recv_sem=recv_sem,
            device_id=device(index), device_id_type=MESH,
        )

    def gather_copy(side, step, kind, u, block, own_other=False):
        return remote(
            others.at[u] if own_other else blocks.at[block, u],
            blocks.at[block, u],
            gather_send.at[side, step, kind, u],
            gather_recv.at[side, step, kind, u],
            ahead(side, 1 if own_other else 2),
        )

    def kv_copy(which, p):
        source, target = ((cached_keys, keys), (cached_values, values))[which]
        part = pl.ds(p * piece, piece)
        return remote(
            source.at[part], target.at[1, part], kv_send.at[which, p], kv_recv.at[which, p], partner
        )

    def order(position):
        return (position % 2, position // 2) if isinstance(position, int) else (lax.rem(position, 2), position // 2)

    def goes_on(side, kind, u, step, last):
        return (step < last) | ((step == last) & ((kind == 1) | (u == side)))

    for load in own_loads + other_loads:
        load.wait()
    for u in range(HALF):
        for kind in range(2):
            for side in SIDES:
                gather_copy(side, 0, kind, u, me, own_other=kind == 1).start()
        if u == HALF - 1:
            for which in range(2):
                for p in range(KV_PIECES):
                    kv_copy(which, p).start()

    for load in kv_loads + tables:
        load.start()
    for table in tables:
        table.wait()
    for owner in range(n):
        source = jnp.int32(0)
        for b in range(n):
            source = jnp.maximum(source, jnp.where(owner_ids[b] == owner, b, 0))
        inverse[owner] = source
    shards = (me, partner)
    bounds = []
    begin = jnp.int32(0)
    for t in range(turns):
        end = begin + turn_lengths[t]
        bounds.append((begin, end, tile_map[t, me], tile_map[t, partner]))
        begin = end

    def prepare(s):
        limit = prefix_len[shards[s]]
        live = lax.broadcasted_iota(jnp.int32, (cache, HD), 0) < limit
        key_all = keys[s].astype(jnp.float32) * scale2
        key_all = jnp.where(live, key_all, jnp.broadcast_to(key_all[0:1, :], (cache, HD)))
        high = key_all.astype(jnp.bfloat16)
        key_rows[s, :, 0:HD] = high
        key_rows[s, :, HD:2 * HD] = (key_all - high.astype(jnp.float32)).astype(jnp.bfloat16)
        value_all = jnp.where(live, values[s].astype(jnp.float32), 0.0)
        value_cols[s, 0:HD, :] = value_all.T.astype(jnp.bfloat16)
        counted = lax.broadcasted_iota(jnp.int32, (COUNT_ROWS, cache), 1) < limit
        value_cols[s, HD:HD + COUNT_ROWS, :] = jnp.where(counted, 1.0, 0.0).astype(jnp.bfloat16)

    lane = lax.broadcasted_iota(jnp.int32, (2, lanes), 1)
    even_row = lax.broadcasted_iota(jnp.int32, (2, lanes), 0) == 0


    def score(s, pairs):
        query = jnp.concatenate(
            [
                blocks[block, u, :, pl.ds(j * HD, HD)]
                for block, u in pairs
                for j in range(per_chunk)
            ],
            axis=0,
        )
        query = jnp.concatenate([query, query], axis=1)
        scores = lax.dot_general(
            key_rows[s], query, (((1,), (1,)), ((), ())), preferred_element_type=jnp.float32
        )
        peak = jnp.max(scores.reshape(cache // 32, 32, scores.shape[1]), axis=0)
        return scores, jnp.max(peak, axis=0, keepdims=True)

    def absorb(s, pairs, scores, peak):
        weights = jnp.exp2(scores - peak).astype(jnp.bfloat16)
        mixed = jnp.dot(value_cols[s], weights, preferred_element_type=jnp.float32)
        total = jnp.maximum(mixed[HD:HD + 1, :], 1.0)
        part = (mixed[0:HD, :] * (1.0 / total)).astype(jnp.bfloat16)
        spread = peak + jnp.log2(total)
        for i, (block, u) in enumerate(pairs):
            partials[s, block, u] = part[:, i * lanes:(i + 1) * lanes]
            spreads[s, block, u] = jnp.broadcast_to(
                spread[:, i * lanes:(i + 1) * lanes], (2, lanes)
            )

    def compute(*units):
        ahead_of = score(*units[0])
        for i, unit in enumerate(units):
            now = ahead_of
            if i + 1 < len(units):
                ahead_of = score(*units[i + 1])
            absorb(*unit, *now)

    def block_at(side, step, kind):
        return place(kind - 2 * step) if side == RIGHT else place(2 * step - kind)

    def pairs_at(step, position):
        kind, u = order(position)
        return [(block_at(side, step, kind), u) for side in SIDES]

    def arrive(step, position, sides=SIDES):
        kind, u = order(position)
        for side in sides:
            block = block_at(side, step, kind)
            gather_copy(side, step - 1, kind, u, block).wait_recv()
            if isinstance(step, int) and step == steps:
                continue

            @pl.when(goes_on(side, kind, u, step, steps - 1))
            def _():
                gather_copy(side, step, kind, u, block).start()

    def sent(step, position):
        kind, u = order(position)
        for side in SIDES:
            gather_copy(side, step, kind, u, me).wait_send()

    own_pairs = [(me, 0), (me, 1)]
    for load in kv_loads:
        load.wait()
    prepare(0)
    compute((0, own_pairs))

    def early_step(it, carry):
        step, first = it // HALF, 2 * lax.rem(it, HALF)
        for position in (first, first + 1):
            arrive(step, position)
        compute(*[(0, pairs_at(step, position)) for position in (first, first + 1)])
        return carry

    lax.fori_loop(HALF, 3 * HALF, early_step, 0)
    for which in range(2):
        for p in range(KV_PIECES):
            kv_copy(which, p).wait_recv()
    prepare(1)
    compute((1, own_pairs))

    def late_step(position, carry):
        arrive(3, position)
        compute(
            (0, pairs_at(3, position)), *[(1, pairs_at(step, position)) for step in range(1, 4)]
        )
        for step in range(1, 4):
            sent(step - 1, position)
        return carry

    lax.fori_loop(0, CHUNKS, late_step, 0)

    def last_step(u):
        units = []
        for kind in range(2):
            sides = SIDES if kind == 1 else (u,)
            arrive(steps, 2 * u + kind, sides)
            pairs = [(block_at(side, steps, kind), u) for side in sides]
            units = units + [(0, pairs), (1, pairs)]
        compute(*units)

    def own_spread(s, even, odd, u):
        spread = jnp.where(even_row, spreads[s, even, u], spreads[s, odd, u])
        row = jnp.where(even_row, even, odd) * rows + lax.rem(lane, rows)
        sees = jnp.zeros((2, lanes), jnp.int32)
        for bound in bounds:
            sees = sees + jnp.where((row >= bound[0]) & (row < bound[1]), bound[2 + s], 0)
        return jnp.where(sees > 0, spread, NEG)

    def part_copy(side, step, kind, u):
        return remote(
            leaving.at[side, step, kind, u],
            arrived.at[side, step, kind, u],
            part_send.at[side, step, kind, u],
            part_recv.at[side, step, kind, u],
            ahead(side, 1 if step == steps - 1 and kind == 1 else 2),
        )

    def spread_copy(side, step, u, kind=0):
        to = step + 1 if kind == 1 else step
        return remote(
            leaving_spread.at[side, step, u],
            arrived_spread.at[side, to, u],
            spread_send.at[side, to, u],
            spread_recv.at[side, to, u],
            ahead(side, 1 if kind == 1 else 2),
        )

    def weights_of(terms):
        top = terms[0]
        for term in terms[1:]:
            top = jnp.maximum(top, term)
        terms = [jnp.exp2(term - top) for term in terms]
        total = terms[0]
        for term in terms[1:]:
            total = total + term
        return [term / total for term in terms], top + jnp.log2(total)

    def mix(kind, sources):
        full = None
        for weight, term in sources:
            term = term.astype(jnp.float32) * weight[kind:kind + 1, :]
            full = term if full is None else full + term
        return full

    def starts(side, kind, u, step):
        return step == 0 or (step == 1 and kind == 0 and u != side)

    def merge_step(step, u):
        blocks_at, shares = [], []
        for side in SIDES:
            far = 2 * (steps - step)
            blocks_of = [inverse[ahead(side, far)], inverse[ahead(side, far - 1)]]
            terms = [own_spread(s, *blocks_of, u) for s in range(2)]
            if step == 0:
                if u != side:
                    terms = [jnp.where(even_row, NEG, term) for term in terms]
            else:
                spread_copy(side, step - 1, u).wait_recv()
                terms.append(arrived_spread[side, step - 1, u])
            weights, spread = weights_of(terms)
            leaving_spread[side, step, u] = spread
            spread_copy(side, step, u).start()
            if step == steps - 1:
                spread_copy(side, step, u, 1).start()
            blocks_at.append(blocks_of)
            shares.append(weights)
        for kind in range(2):
            for side in SIDES:
                if step == 0 and kind == 0 and u != side:
                    continue
                come = [(shares[side][s], partials[s, blocks_at[side][kind], u]) for s in range(2)]
                if not starts(side, kind, u, step):
                    part_copy(side, step - 1, kind, u).wait_recv()
                    come.append((shares[side][2], arrived[side, step - 1, kind, u]))
                leaving[side, step, kind, u] = mix(kind, come).astype(jnp.bfloat16)
                part_copy(side, step, kind, u).start()

    for u in range(HALF):
        last_step(u)
        merge_step(0, u)
    for step in range(1, steps):
        for u in range(HALF):
            merge_step(step, u)

    def settle(merge_steps):
        for side in SIDES:
            for u in range(HALF):
                for step in merge_steps:
                    for kind in range(2):
                        if step or kind == 1 or u == side:
                            part_copy(side, step, kind, u).wait_send()
                    spread_copy(side, step, u).wait_send()
                    if step == steps - 1:
                        spread_copy(side, step, u, 1).wait_send()

    for side in SIDES:
        for u in range(HALF):
            for kind in range(2):
                if goes_on(side, kind, u, steps - 1, steps - 1):
                    gather_copy(side, steps - 1, kind, u, me).wait_send()
    for which in range(2):
        for p in range(KV_PIECES):
            kv_copy(which, p).wait_send()
    settle(range(steps - 1))

    source = inverse[me]
    for u in range(HALF):
        for side in SIDES:
            spread_copy(side, steps - 1, u).wait_recv()
            spread_copy(side, steps - 1, u, 1).wait_recv()
        own_weights, _ = weights_of(
            [own_spread(s, source, source, u) for s in range(2)]
            + [arrived_spread[side, steps - 1, u] for side in SIDES]
        )
        other_weights, _ = weights_of([arrived_spread[side, steps, u] for side in SIDES])
        for kind in range(2):
            for side in SIDES:
                part_copy(side, steps - 1, kind, u).wait_recv()
            come = [arrived[side, steps - 1, kind, u] for side in SIDES]
            if kind == 0:
                come = [partials[s, source, u] for s in range(2)] + come
            share = own_weights if kind == 0 else other_weights
            full = mix(kind, zip(share, come)).T.astype(jnp.bfloat16)
            c = HALF * (parity if kind == 0 else 1 - parity) + u
            for j in range(per_chunk):
                at = pl.ds(pl.multiple_of(c * width + j * HD, HD), HD)
                result[:, at] = full[j * rows:(j + 1) * rows]

    settle(range(steps - 1, steps))


def per_device(queries, cached_keys, cached_values, turn_lengths, tile_map, prefix_len, owner_ids):
    n = lax.axis_size("ctx")
    rows, columns = queries.shape
    cache = cached_keys.shape[0]
    width = columns // CHUNKS
    steps = n // 4
    lanes = rows * width // HD
    hbm = pl.BlockSpec(memory_space=pl.ANY)
    dma = pltpu.SemaphoreType.DMA
    tables = (turn_lengths, tile_map, prefix_len, owner_ids)
    return pl.pallas_call(
        kernel,
        out_shape=pltpu.VMEM((rows, columns), jnp.bfloat16),
        in_specs=[hbm] * 7,
        out_specs=pl.BlockSpec(memory_space=pltpu.VMEM),
        scratch_shapes=[pltpu.SMEM(table.shape, jnp.int32) for table in tables]
        + [
            pltpu.SMEM((n,), jnp.int32),
            pltpu.VMEM((HALF, rows, width), jnp.bfloat16),
            pltpu.VMEM((n, HALF, rows, width), jnp.bfloat16),
            pltpu.VMEM((2, n, HALF, HD, lanes), jnp.bfloat16),
            pltpu.VMEM((2, n, HALF, 2, lanes), jnp.float32),
            pltpu.VMEM((2, cache, HD), jnp.bfloat16),
            pltpu.VMEM((2, cache, HD), jnp.bfloat16),
            pltpu.VMEM((2, cache, 2 * HD), jnp.bfloat16),
            pltpu.VMEM((2, HD + COUNT_ROWS, cache), jnp.bfloat16),
            pltpu.VMEM((2, steps, 2, HALF, HD, lanes), jnp.bfloat16),
            pltpu.VMEM((2, steps, 2, HALF, HD, lanes), jnp.bfloat16),
            pltpu.VMEM((2, steps + 1, HALF, 2, lanes), jnp.float32),
            pltpu.VMEM((2, steps, HALF, 2, lanes), jnp.float32),
            dma((CHUNKS,)),
            dma((len(tables),)),
            dma((2,)),
            dma((2, KV_PIECES)),
            dma((2, KV_PIECES)),
            dma((2, steps, 2, HALF)),
            dma((2, steps, 2, HALF)),
            dma((2, steps, 2, HALF)),
            dma((2, steps, 2, HALF)),
            dma((2, steps + 1, HALF)),
            dma((2, steps + 1, HALF)),
        ],
        compiler_params=pltpu.CompilerParams(
            collective_id=0, has_side_effects=True, vmem_limit_bytes=VMEM_BYTES
        ),
        cost_estimate=pl.CostEstimate(
            flops=4 * n * rows * columns * cache,
            bytes_accessed=1 << 20,
            transcendentals=n * rows * columns * cache // HD,
        ),
    )(*[pltpu.with_memory_space_constraint(x, pltpu.HBM) for x in (queries, cached_keys, cached_values, *tables)])


VMEM_BYTES = 48 * 1024 * 1024


def solution(mesh):
    return jax.shard_map(
        per_device,
        mesh=mesh,
        in_specs=(
            P(("pack", "ctx"), "head"),
            P(("pack", "ctx"), "head"),
            P(("pack", "ctx"), "head"),
            P("pack"),
            P("pack", None),
            P("pack"),
            P("pack"),
        ),
        out_specs=P(("pack", "ctx"), "head"),
        check_vma=False,
    )
```
